32 devices in a mesh: tm: 4 (over y, x), space: 2 (over core), dp: 4 (over z).
Axes of the slice: x: 2, y: 2, z: 4, core: 2. Of those that a mesh axis runs over, the one named last changes fastest.
Arguments:
- projected: bfloat16 [16, 1024, 3, 40, 128], P(('dp', 'tm'), None, None, 'space'), parts along dimension 0, may hold values from -256 to 256
- q_gain: float32 [40, 128], P('space'), may hold values from 0.1 to 1.9
- k_gain: float32 [40, 128], P('space'), may hold values from 0.1 to 1.9
- head_weight: float32 [40, 128], P('space'), may hold values from -0.078125 to 0.078125
- step_scale: float32 [4, 40, 128], P(None, 'space'), may hold values from 0.5 to 1.5
- timestep: int32 [16], P('dp'), parts along dimension 0, may hold values from 0 to 3
- frame_count: int32 [4096], P('dp'), parts along dimension 0, may hold values from 1 to 4
Outputs:
- logits: float32 [16, 1024], P(('dp', 'tm'), 'space'), parts along dimension 0
The draws below stay inside these ranges and needn't reach their ends.
There are 4 independent parts, one for each index of `dp`. The reference program is written for one: setup_inputs(seed, part) draws one part's arguments, and reference() takes and returns one part's arrays. A program takes and returns all parts, laid end to end along the dimension named above; an argument that names none is the same for every part. Nothing has to cross between parts.
All inputs are finite; a program needn't handle non-finite values.
Results may differ from the reference program's by a relative error of at most 0.01.
Values may be sent and summed in bfloat16 or wider, within the bound.
No kernel may reach another device: no remote copies, remote signals or barrier semaphores. Data moves between devices by JAX's collectives and lax.ppermute only.
A program may use at most 128 MiB of HBM per device.

```python
import math
import jax
import jax.numpy as jnp
from jax import lax

HEADS = 40
HEAD = 128
PIXELS = 1024
STEPS = 4
FRAMES = 4


def draw_projected(key, part):
    key = jax.random.fold_in(key, 17)
    keys = jax.random.split(key, 3)
    shape = (FRAMES, PIXELS, 3, HEADS, HEAD)
    ramp = 3.0 ** (jnp.arange(HEADS, dtype=jnp.float32) / max(HEADS - 1, 1))
    ramp = ramp[None, None, None, :, None]
    base = jnp.clip(jax.random.normal(keys[0], shape, jnp.float32), -3.0, 3.0)
    row_scale = jnp.exp(jax.random.uniform(keys[1], (FRAMES, PIXELS, 3, 1, 1), jnp.float32, math.log(0.3), math.log(3.0)))
    column_scale = jnp.exp(jax.random.uniform(keys[2], (1, 1, 3, HEADS, HEAD), jnp.float32, math.log(0.3), math.log(3.0))) * ramp
    field = base * row_scale * column_scale
    return field.astype(jnp.bfloat16)


def place_ends(result, own_key, least, high):
    index_at = [jax.random.randint(jax.random.fold_in(own_key, axis), (), 0, length) for axis, length in enumerate(result.shape)]
    widest = result.shape.index(max(result.shape))
    next_to = index_at[:widest] + [(index_at[widest] + 1) % result.shape[widest]] + index_at[widest + 1:]
    return result.at[tuple(index_at)].set(least).at[tuple(next_to)].set(high)


def block_scale(key, extent, pieces, low, top_value):
    loudness, own = 1.0, jax.random.fold_in(key, 6)
    for axis_at, parts in pieces:
        draws = jnp.exp(jax.random.uniform(jax.random.fold_in(own, axis_at), (parts,), jnp.float32, low / len(pieces), top_value / len(pieces)))
        loudness = loudness * jnp.repeat(draws, extent[axis_at] // parts).reshape([-1 if axis == axis_at else 1 for axis in range(len(extent))])
    return loudness


def bell_draw(own_key, dims, scale, reach, cuts=(), held_as=jnp.bfloat16):
    drawn = scale * jax.random.normal(own_key, dims, jnp.float32)
    if cuts:
        drawn = drawn * block_scale(own_key, dims, cuts, -0.22, 0.18)
    return jnp.clip(drawn, -reach, reach).astype(held_as)


def setup_inputs(seed: int = 0, part: int = 0) -> dict:
    splits = jax.random.split(jax.random.key(seed), 8)
    part_keys = jax.random.split(jax.random.fold_in(splits[7], part), 8)
    return {
        "projected": draw_projected(jax.random.fold_in(jax.random.fold_in(splits[7], part), 71), part),
        "q_gain": jnp.clip(1.0 + 0.18 * jax.random.normal(splits[1], (HEADS, HEAD), jnp.float32), 0.1, 1.9),
        "k_gain": jnp.clip(1.0 + 0.18 * jax.random.normal(splits[2], (HEADS, HEAD), jnp.float32), 0.1, 1.9),
        "head_weight": bell_draw(splits[3], (HEADS, HEAD), (HEADS * HEAD) ** -0.5, 0.078125, ((0, 2),), jnp.float32),
        "step_scale": jnp.clip(0.5 + 1.0 * jax.random.uniform(splits[4], (STEPS, HEADS, HEAD), jnp.float32) ** block_scale(splits[4], (STEPS, HEADS, HEAD), ((1, 2),), -0.2, 0.2), 0.5, 1.5),
        "timestep": place_ends(jax.random.randint(part_keys[5], (FRAMES,), 0, STEPS), jax.random.fold_in(part_keys[5], 1), 0, STEPS - 1).astype(jnp.int32),
        "frame_count": place_ends(jax.random.randint(part_keys[6], (PIXELS,), 1, FRAMES + 1), jax.random.fold_in(part_keys[6], 1), 1, FRAMES).astype(jnp.int32),
    }


epsilon = 1e-06

def reference(projected, q_gain, k_gain, head_weight, step_scale, timestep, frame_count):
    scaling = HEAD ** (-0.5)
    channels = HEADS * HEAD

    def normalize(features_in, gain_row):
        wide_rows = features_in.astype(jnp.float32)
        sum_squares = lax.optimization_barrier(jnp.sum(wide_rows * wide_rows, axis=(1, 2), keepdims=True))
        return (wide_rows * lax.rsqrt(sum_squares / channels + epsilon) * gain_row).astype(jnp.bfloat16)

    def spatial_head(trio):
        query_head, key_head, value_head = trio
        scores = jnp.dot(query_head, key_head.T, preferred_element_type=jnp.float32) * scaling
        row_max = lax.optimization_barrier(jnp.max(scores, axis=1, keepdims=True))
        exponent = jnp.exp(scores - row_max)
        weights = (exponent / lax.optimization_barrier(jnp.sum(exponent, axis=1, keepdims=True))).astype(jnp.bfloat16)
        return jnp.dot(weights, value_head, preferred_element_type=jnp.float32).astype(jnp.bfloat16)

    def frame_pass(frame_rows):
        q_heads = jnp.swapaxes(normalize(frame_rows[:, 0], q_gain), 0, 1)
        k_heads = jnp.swapaxes(normalize(frame_rows[:, 1], k_gain), 0, 1)
        v_heads = jnp.swapaxes(frame_rows[:, 2], 0, 1)
        spatial = lax.map(spatial_head, (q_heads, k_heads, v_heads))
        return (q_heads, k_heads, spatial)
    q_all, k_all, spatial_all = lax.map(frame_pass, projected)
    spatial_all = lax.optimization_barrier(spatial_all)
    live_frames = jnp.arange(FRAMES, dtype=jnp.int32)[None, :] < frame_count.astype(jnp.int32)[:, None]

    def temporal_head(trio):
        query_head, key_head, value_head = trio
        scores = jnp.einsum('fpe,gpe->pfg', query_head.astype(jnp.float32), key_head.astype(jnp.float32)) * scaling
        scores = jnp.where(live_frames[:, None, :], scores, -1e+30)
        row_max = lax.optimization_barrier(jnp.max(scores, axis=2, keepdims=True))
        exponent = jnp.exp(scores - row_max)
        weights = (exponent / lax.optimization_barrier(jnp.sum(exponent, axis=2, keepdims=True))).astype(jnp.bfloat16)
        return jnp.einsum('pfg,gpe->fpe', weights.astype(jnp.float32), value_head.astype(jnp.float32)).astype(jnp.bfloat16)
    temporal_all = lax.map(temporal_head, (jnp.swapaxes(q_all, 0, 1), jnp.swapaxes(k_all, 0, 1), jnp.swapaxes(spatial_all, 0, 1)))
    temporal_all = lax.optimization_barrier(temporal_all)
    frame_scales = jnp.take(step_scale, timestep.astype(jnp.int32), axis=0)
    frame_scales = jnp.swapaxes(frame_scales, 0, 1)
    combined = jnp.swapaxes(spatial_all, 0, 1).astype(jnp.float32) + temporal_all.astype(jnp.float32)
    modulated = combined * frame_scales[:, :, None, :]
    dot_total = lax.optimization_barrier(jnp.sum(modulated * head_weight[:, None, None, :], axis=(0, 3)))
    square_total = lax.optimization_barrier(jnp.sum(modulated * modulated, axis=(0, 3)))
    return dot_total * lax.rsqrt(square_total / channels + epsilon)
```

```python
import functools

import jax
import jax.numpy as jnp
from jax import lax
from jax.experimental import pallas as pl
from jax.experimental.pallas import tpu as pltpu
from jax.sharding import PartitionSpec as P

HEADS = 40
HEAD = 128
CHANNELS = HEADS * HEAD
EPSILON = 1e-06
LOG2E = 1.4426950408889634
SCALE2 = HEAD ** (-0.5) * LOG2E
MASKED = -1e30
NT = (((1,), (1,)), ((), ()))
VMEM_LIMIT = 48 * 1024 * 1024


def lane_sums(acc):
    pieces = []
    for start in range(0, acc.shape[0], HEAD):
        pieces.append(jnp.sum(acc[start : start + HEAD].T, axis=0, keepdims=True))
    return jnp.concatenate(pieces, axis=1)


def spread_rows(row):
    pieces = []
    for start in range(0, row.shape[1], HEAD):
        piece = jnp.broadcast_to(row[:, start : start + HEAD], (HEAD, HEAD))
        pieces.append(piece.T)
    return jnp.concatenate(pieces, axis=0)


def store_shares(count_ref, rank_ref, frames_ref=None):
    shares, width = rank_ref.shape
    lines = width // HEAD
    many = jnp.where(count_ref[...] >= 2, 1.0, 0.0)
    row = lax.broadcasted_iota(jnp.int32, (HEAD, HEAD), 0)
    column = lax.broadcasted_iota(jnp.int32, (HEAD, HEAD), 1)
    upto = jnp.dot(
        many, jnp.where(row <= column, 1.0, 0.0), preferred_element_type=jnp.float32
    )
    lane = lax.broadcasted_iota(jnp.int32, (1, HEAD), 1).astype(jnp.float32)
    for share in range(shares):
        total = jnp.zeros((1, 1), jnp.float32)
        before = []
        for line in range(share * lines, (share + 1) * lines):
            before.append(upto[line : line + 1] - many[line : line + 1] + total)
            total = total + upto[line : line + 1, HEAD - 1 :]
        for i in range(lines):
            line = share * lines + i
            later = total + (lane + float(i * HEAD)) - before[i]
            rank = jnp.where(many[line : line + 1] > 0.5, before[i], later)
            here = (slice(share, share + 1), slice(i * HEAD, (i + 1) * HEAD))
            rank_ref[here] = rank.astype(jnp.int32)
            if frames_ref is not None:
                frames_ref[here] = count_ref[line : line + 1].astype(jnp.float32)


def picks(rank_ref, owner, each, first, size):
    width = rank_ref.shape[1]
    place = lax.broadcasted_iota(jnp.int32, (size, width), 0) + first
    return rank_ref[pl.ds(lax.div(owner, each), 1), :] == place * each + lax.rem(owner, each)


def gather_kernel(slots_ref, count_ref, *refs, offsets, each, first, with_sums):
    number = len(offsets)
    sources = 2 if with_sums else 2 * number
    sources, refs = refs[:sources], refs[sources:]
    outs, refs = refs[:number], refs[number:]
    if with_sums:
        out_ref, rank_ref, pick_ref, acc_ref = refs
    else:
        rank_ref, pick_ref = refs
    step = pl.program_id(0)
    size = outs[0].shape[2]

    @pl.when(step == 0)
    def _():
        store_shares(count_ref, rank_ref)
        for i, offset in enumerate(offsets):
            hit = picks(rank_ref, slots_ref[offset], each, first, size)
            pick_ref[i] = jnp.where(hit, 1.0, 0.0).astype(jnp.bfloat16)
        if with_sums:
            acc_ref[...] = jnp.zeros_like(acc_ref)

    width = rank_ref.shape[1]
    for i, offset in enumerate(offsets):
        start = pl.multiple_of(lax.div(slots_ref[offset], each) * width, width)
        for h in range(outs[i].shape[1]):
            if with_sums:
                rows = [source[0, h, pl.ds(start, width), :] for source in sources]
            else:
                rows = [source[0, h] for source in sources[2 * i : 2 * i + 2]]
            rows = jnp.concatenate(rows, axis=1)
            rows = jnp.dot(pick_ref[i], rows, preferred_element_type=jnp.float32)
            rows = rows.astype(jnp.bfloat16)
            outs[i][0, h] = rows[:, :HEAD]
            outs[i][1, h] = rows[:, HEAD:]
    if with_sums:
        for which in range(2):
            sums = acc_ref[which]
            for h in range(sources[which].shape[1]):
                wide = sources[which][0, h].astype(jnp.float32)
                sums = sums + wide * wide
            acc_ref[which] = sums

        @pl.when(step == pl.num_programs(0) - 1)
        def _():
            for which in range(2):
                out_ref[which : which + 1] = lane_sums(acc_ref[which])


def gather(slots, counts, x, offsets, each, shares, first, size, at, heads, with_sums=False):
    pixels = x.shape[2]
    step = max(i for i in range(1, 6) if heads % i == 0 and at % i == 0)
    step = step // 2 if step == heads and step % 2 == 0 else step
    skip = at // step
    width = pixels // shares

    def source(which, offset):
        return pl.BlockSpec(
            (1, step, width, HEAD), lambda h, s: (which, skip + h, lax.div(s[offset], each), 0)
        )

    in_specs = [pl.BlockSpec(counts.shape, lambda h, s: (0, 0))]
    if not with_sums:
        in_specs += [source(which, offset) for offset in offsets for which in range(2)]
    out_specs = [pl.BlockSpec((2, step, size, HEAD), lambda h, s: (0, h, 0, 0))] * len(offsets)
    out_shape = [jax.ShapeDtypeStruct((2, heads, size, HEAD), jnp.bfloat16)] * len(offsets)
    scratch = [
        pltpu.VMEM((shares, width), jnp.int32),
        pltpu.VMEM((len(offsets), size, width), jnp.bfloat16),
    ]
    if with_sums:
        for which in range(2):
            in_specs.append(
                pl.BlockSpec(
                    (1, step, pixels, HEAD), lambda h, s, which=which: (which, skip + h, 0, 0)
                )
            )
        out_specs.append(pl.BlockSpec((2, pixels), lambda h, s: (0, 0)))
        out_shape.append(jax.ShapeDtypeStruct((2, pixels), jnp.float32))
        scratch.append(pltpu.VMEM((2, pixels, HEAD), jnp.float32))
    return pl.pallas_call(
        functools.partial(
            gather_kernel, offsets=tuple(offsets), each=each, first=first, with_sums=with_sums
        ),
        grid_spec=pltpu.PrefetchScalarGridSpec(
            num_scalar_prefetch=1,
            grid=(heads // step,),
            in_specs=in_specs,
            out_specs=out_specs,
            scratch_shapes=scratch,
        ),
        out_shape=out_shape,
        compiler_params=pltpu.CompilerParams(vmem_limit_bytes=VMEM_LIMIT),
        cost_estimate=pl.CostEstimate(
            flops=4 * heads * pixels * HEAD,
            bytes_accessed=4 * heads * (len(offsets) * size + pixels) * HEAD,
            transcendentals=0,
        ),
        name="gather_sums" if with_sums else "gather",
    )(slots, counts, *[x] * (len(in_specs) - 1))


def spatial_kernel(
    slots_ref, count_ref, q_ref, k_ref, v_ref, factor_ref, qg_ref, kg_ref, *rest, count, each
):
    outs, rest = rest[:count], rest[count:]
    fq_ref, fk_ref, qn_ref, kn_ref, ve_ref, rank_ref, pick_ref = rest
    width = rank_ref.shape[1]

    @pl.when(pl.program_id(0) == 0)
    def _():
        fq_ref[...] = spread_rows(factor_ref[0:1])
        fk_ref[...] = spread_rows(factor_ref[1:2])
        ve_ref[:, :, HEAD:] = jnp.ones((ve_ref.shape[0], ve_ref.shape[1], HEAD), jnp.bfloat16)
        store_shares(count_ref, rank_ref)
        for slot in range(count):
            hit = picks(rank_ref, slots_ref[slot], each, 0, pick_ref.shape[1])
            pick_ref[slot] = jnp.where(hit, 1.0, 0.0).astype(jnp.bfloat16)

    many = q_ref.shape[1]
    for h in range(many):
        qn = q_ref[0, h].astype(jnp.float32) * fq_ref[...] * qg_ref[h]
        qn_ref[:, h * HEAD : (h + 1) * HEAD] = qn.astype(jnp.bfloat16)
        kn = k_ref[0, h].astype(jnp.float32) * fk_ref[...] * kg_ref[h]
        kn_ref[h] = kn.astype(jnp.bfloat16)
        ve_ref[h, :, :HEAD] = v_ref[0, h]
    for slot in range(count):
        start = pl.multiple_of(lax.div(slots_ref[slot], each) * width, width)
        picked = jnp.dot(
            pick_ref[slot], qn_ref[pl.ds(start, width), :], preferred_element_type=jnp.float32
        ).astype(jnp.bfloat16)
        for h in range(many):
            qn = picked[:, h * HEAD : (h + 1) * HEAD]
            s = lax.dot_general(qn, kn_ref[h], NT, preferred_element_type=jnp.float32)
            top = jnp.max(s, axis=1, keepdims=True)
            p = jnp.exp2(s * SCALE2 - top * SCALE2).astype(jnp.bfloat16)
            o = jnp.dot(p, ve_ref[h], preferred_element_type=jnp.float32)
            outs[slot][h] = (o[:, :HEAD] / o[:, HEAD:]).astype(jnp.bfloat16)


def spatial(slots, counts, x, factors, q_gain, k_gain, first, size, count, each, shares):
    pixels = x.shape[2]
    block, width = pixels // count, pixels // shares

    def rows(which):
        return pl.BlockSpec((1, step, pixels, HEAD), lambda h, s: (which, skip + h, 0, 0))

    step = 2 if size % 2 == 0 and first % 2 == 0 else 1
    skip = first // step
    gain = pl.BlockSpec((step, 1, HEAD), lambda h, s: (skip + h, 0, 0))
    return pl.pallas_call(
        functools.partial(spatial_kernel, count=count, each=each),
        grid_spec=pltpu.PrefetchScalarGridSpec(
            num_scalar_prefetch=1,
            grid=(size // step,),
            in_specs=[
                pl.BlockSpec(counts.shape, lambda h, s: (0, 0)),
                rows(0),
                rows(1),
                rows(2),
                pl.BlockSpec((2, pixels), lambda h, s: (0, 0)),
                gain,
                gain,
            ],
            out_specs=[pl.BlockSpec((step, block, HEAD), lambda h, s: (h, 0, 0))] * count,
            scratch_shapes=[
                pltpu.VMEM((pixels, HEAD), jnp.float32),
                pltpu.VMEM((pixels, HEAD), jnp.float32),
                pltpu.VMEM((pixels, step * HEAD), jnp.bfloat16),
                pltpu.VMEM((step, pixels, HEAD), jnp.bfloat16),
                pltpu.VMEM((step, pixels, 2 * HEAD), jnp.bfloat16),
                pltpu.VMEM((shares, width), jnp.int32),
                pltpu.VMEM((count, block, width), jnp.bfloat16),
            ],
        ),
        out_shape=[jax.ShapeDtypeStruct((size, block, HEAD), jnp.bfloat16)] * count,
        compiler_params=pltpu.CompilerParams(vmem_limit_bytes=VMEM_LIMIT),
        cost_estimate=pl.CostEstimate(
            flops=8 * size * pixels * pixels * HEAD,
            bytes_accessed=8 * size * pixels * HEAD,
            transcendentals=size * pixels * pixels,
        ),
        name="spatial_attention",
    )(slots, counts, x, x, x, factors, q_gain, k_gain)


def far_sums_kernel(*refs):
    far, (out_ref, acc_ref) = refs[:-2], refs[-2:]
    head = pl.program_id(0)
    block = far[0].shape[2]

    @pl.when(head == 0)
    def _():
        acc_ref[...] = jnp.zeros_like(acc_ref)

    for i, ref in enumerate(far):
        which, at = i % 2, i // 2 * block
        sums = acc_ref[which, at : at + block]
        for h in range(ref.shape[1]):
            wide = ref[0, h].astype(jnp.float32)
            sums = sums + wide * wide
        acc_ref[which, at : at + block] = sums

    @pl.when(head == pl.num_programs(0) - 1)
    def _():
        for which in range(2):
            out_ref[which : which + 1] = lane_sums(acc_ref[which])


def far_sums(far, heads):
    block = far[0][0].shape[2]
    rows = len(far) // 2 * block
    step = max(i for i in range(1, 6) if all(n % i == 0 for n in (heads, *[f[2] for f in far])))
    return pl.pallas_call(
        far_sums_kernel,
        grid=(heads // step,),
        in_specs=[
            pl.BlockSpec(
                (1, step, block, HEAD),
                lambda h, place=place, skip=at // step: (place, skip + h, 0, 0),
            )
            for _, place, at in far
        ],
        out_specs=pl.BlockSpec((2, rows), lambda h: (0, 0)),
        out_shape=jax.ShapeDtypeStruct((2, rows), jnp.float32),
        scratch_shapes=[pltpu.VMEM((2, rows, HEAD), jnp.float32)],
        compiler_params=pltpu.CompilerParams(vmem_limit_bytes=VMEM_LIMIT),
        cost_estimate=pl.CostEstimate(
            flops=4 * heads * rows * HEAD, bytes_accessed=4 * heads * rows * HEAD, transcendentals=0
        ),
        name="far_sums",
    )(*[array for array, _, _ in far])


def weights_kernel(
    slots_ref, count_ref, factor_ref, frame_ref, qg_ref, kg_ref, *rest, each, first, part
):
    far, (out_ref, fq_ref, fk_ref, rank_ref, frames_ref, bias_ref) = rest[:-6], rest[-6:]
    count = len(far) // 2
    size = far[0].shape[2]
    wide = count * part

    @pl.when(pl.program_id(0) == 0)
    def _():
        fq_ref[...] = spread_rows(factor_ref[0:1])
        fk_ref[...] = spread_rows(factor_ref[1:2])
        store_shares(count_ref, rank_ref, frames_ref)
        me = slots_ref[0]
        frames = frames_ref[pl.ds(lax.div(me, each), 1), :]
        hit = picks(rank_ref, me, each, first, size)
        frames = jnp.sum(jnp.where(hit, frames, 0.0), axis=1, keepdims=True)
        row = lax.broadcasted_iota(jnp.int32, (wide, wide), 0)
        column = lax.broadcasted_iota(jnp.int32, (wide, wide), 1)
        same = ((row - column) & (part - 1)) == 0
        for j in range(size // part):
            held = jnp.concatenate([frames[j * part : (j + 1) * part]] * count, axis=0)
            live = jnp.where(frame_ref[...] < held, 0.0, MASKED)
            bias_ref[j] = jnp.where(same, live, MASKED)

    def normal(which, factor, gain, at):
        pieces = []
        for slot in range(count):
            rows = far[2 * slot + which][0, 0, at : at + part].astype(jnp.float32)
            rows = rows * factor[slot * size + at : slot * size + at + part] * gain
            pieces.append(rows.astype(jnp.bfloat16))
        return jnp.concatenate(pieces, axis=0)

    for j in range(size // part):
        qn = normal(0, fq_ref, qg_ref[0], j * part)
        kn = normal(1, fk_ref, kg_ref[0], j * part)
        s = lax.dot_general(qn, kn, NT, preferred_element_type=jnp.float32) * SCALE2 + bias_ref[j]
        e = jnp.exp2(s - jnp.max(s, axis=1, keepdims=True))
        out_ref[0, j] = (e * (1.0 / jnp.sum(e, axis=1, keepdims=True))).astype(jnp.bfloat16)


def position_factors(parts):
    sums = functools.reduce(jnp.add, [far_sums(far, heads) for far, heads in parts])
    factors = lax.rsqrt(lax.psum(sums, "space") / CHANNELS + EPSILON)
    return jnp.pad(factors, ((0, 0), (0, -factors.shape[1] % HEAD)))


def temporal_weights(
    slots, counts, factors, far, q_gain, k_gain, each, shares, first, part, start, heads
):
    count = len(far) // 2
    size = far[0][0].shape[2]
    rows, wide, subs = count * size, count * part, size // part
    width = counts.size // shares
    padded = factors.shape[1]
    frame = jnp.repeat(slots, part)[None, :].astype(jnp.float32)
    gain = pl.BlockSpec((1, 1, HEAD), lambda h, s: (start + h, 0, 0))
    return pl.pallas_call(
        functools.partial(weights_kernel, each=each, first=first, part=part),
        grid_spec=pltpu.PrefetchScalarGridSpec(
            num_scalar_prefetch=1,
            grid=(heads,),
            in_specs=[
                pl.BlockSpec(counts.shape, lambda h, s: (0, 0)),
                pl.BlockSpec((2, padded), lambda h, s: (0, 0)),
                pl.BlockSpec((1, wide), lambda h, s: (0, 0)),
                gain,
                gain,
            ]
            + [
                pl.BlockSpec(
                    (1, 1, size, HEAD), lambda h, s, place=place, at=at: (place, at + h, 0, 0)
                )
                for _, place, at in far
            ],
            out_specs=pl.BlockSpec((1, subs, wide, wide), lambda h, s: (h, 0, 0, 0)),
            scratch_shapes=[
                pltpu.VMEM((padded, HEAD), jnp.float32),
                pltpu.VMEM((padded, HEAD), jnp.float32),
                pltpu.VMEM((shares, width), jnp.int32),
                pltpu.VMEM((shares, width), jnp.float32),
                pltpu.VMEM((subs, wide, wide), jnp.float32),
            ],
        ),
        out_shape=jax.ShapeDtypeStruct((heads, subs, wide, wide), jnp.bfloat16),
        compiler_params=pltpu.CompilerParams(vmem_limit_bytes=VMEM_LIMIT),
        cost_estimate=pl.CostEstimate(
            flops=2 * heads * rows * wide * HEAD,
            bytes_accessed=4 * heads * rows * HEAD + 2 * heads * rows * wide,
            transcendentals=heads * rows * wide,
        ),
        name="temporal_weights",
    )(slots, counts, factors, frame, q_gain, k_gain, *[array for array, _, _ in far])


def mix_kernel(slots_ref, count_ref, scale_ref, weight_ref, *rest, count, each, part, more):
    mixed, rest = rest[:count], rest[count:]
    weights, rest = rest[: -(count + 3 + more * count)], rest[-(count + 3 + more * count) :]
    before, rest = rest[: more * count], rest[more * count :]
    outs, (dot_ref, square_ref, rank_ref) = rest[:count], rest[count:]
    head = pl.program_id(0)
    block = mixed[0].shape[1]

    @pl.when(head == 0)
    def _():
        dot_ref[...] = jnp.zeros_like(dot_ref)
        square_ref[...] = jnp.zeros_like(square_ref)
        store_shares(count_ref, rank_ref)

    subs = [(ref, j) for ref in weights for j in range(ref.shape[1])]
    for sub, (p_ref, j) in enumerate(subs):
        at = sub * part
        dots = [dot_ref[slot, at : at + part] for slot in range(count)]
        squares = [square_ref[slot, at : at + part] for slot in range(count)]
        for h in range(p_ref.shape[0]):
            o = jnp.concatenate([mixed[slot][h, at : at + part] for slot in range(count)], axis=0)
            t = jnp.dot(p_ref[h, j], o, preferred_element_type=jnp.float32).astype(jnp.bfloat16)
            both = o.astype(jnp.float32) + t.astype(jnp.float32)
            for slot in range(count):
                m = both[slot * part : (slot + 1) * part] * scale_ref[h, slot : slot + 1]
                dots[slot] = dots[slot] + m * weight_ref[h]
                squares[slot] = squares[slot] + m * m
        for slot in range(count):
            dot_ref[slot, at : at + part] = dots[slot]
            square_ref[slot, at : at + part] = squares[slot]

    @pl.when(head == pl.num_programs(0) - 1)
    def _():
        hit = picks(rank_ref, slots_ref[0], each, 0, block)
        for i, out in enumerate(outs):
            for which, ref in enumerate((dot_ref, square_ref)):
                sums = jnp.sum(ref[slots_ref[count + i]], axis=1, keepdims=True)
                sums = jnp.sum(jnp.where(hit, sums, 0.0), axis=0, keepdims=True)
                if more:
                    sums = before[i][which : which + 1] + sums
                out[which : which + 1] = sums


def mix(slots, counts, weights, scales, weight, before, mixed, first, each, shares, part):
    count = len(mixed)
    size, block, _ = mixed[0].shape
    wide = count * part
    rows = count * block
    width = counts.size // shares
    step = max(i for i in range(1, 6) if size % i == 0 and first % i == 0)
    skip = first // step
    out = pl.BlockSpec((2, width), lambda h, s: (0, 0))
    return pl.pallas_call(
        functools.partial(mix_kernel, count=count, each=each, part=part, more=len(before) // count),
        grid_spec=pltpu.PrefetchScalarGridSpec(
            num_scalar_prefetch=1,
            grid=(size // step,),
            in_specs=[
                pl.BlockSpec(counts.shape, lambda h, s: (0, 0)),
                pl.BlockSpec((step, count, HEAD), lambda h, s: (skip + h, 0, 0)),
                pl.BlockSpec((step, 1, HEAD), lambda h, s: (skip + h, 0, 0)),
            ]
            + [pl.BlockSpec((step, block, HEAD), lambda h, s: (h, 0, 0))] * count
            + [
                pl.BlockSpec(
                    (step, *p.shape[1:]),
                    lambda h, s, skip=(first - at) // step: (skip + h, 0, 0, 0),
                )
                for p, at in weights
            ]
            + [out] * len(before),
            out_specs=[out] * count,
            scratch_shapes=[
                pltpu.VMEM((count, block, HEAD), jnp.float32),
                pltpu.VMEM((count, block, HEAD), jnp.float32),
                pltpu.VMEM((shares, width), jnp.int32),
            ],
        ),
        out_shape=[jax.ShapeDtypeStruct((2, width), jnp.float32)] * count,
        compiler_params=pltpu.CompilerParams(vmem_limit_bytes=VMEM_LIMIT),
        cost_estimate=pl.CostEstimate(
            flops=2 * size * rows * wide * HEAD,
            bytes_accessed=2 * size * rows * (HEAD + wide),
            transcendentals=0,
        ),
        name="temporal_mix",
    )(slots, counts, scales, weight, *mixed, *[p for p, _ in weights], *before)


def on_device(
    projected, q_gain, k_gain, head_weight, step_scale, timestep, frame_count, *, count, shares
):
    x = jnp.transpose(projected[0], (1, 2, 0, 3))
    heads, pixels = x.shape[1], x.shape[2]
    block, width, each = pixels // count, pixels // shares, count // shares
    part = 16
    sure = min(block, -(-13 * block // (16 * part)) * part)
    me = lax.axis_index("tm")
    slots = me ^ jnp.arange(count, dtype=jnp.int32)
    counts = frame_count.reshape(pixels // HEAD, HEAD)
    gains = (q_gain[:, None, :], k_gain[:, None, :])

    def swap(value, offset):
        return lax.ppermute(value, "tm", [(i, i ^ offset) for i in range(count)])

    first = heads * 4 // 5 if heads % 20 == 0 else heads
    ranges = [(at, size) for at, size in ((0, first), (first, heads - first)) if size]
    diagonal = {}
    after = slots
    for at, size in reversed(ranges):
        (piece,) = gather(after, counts, x, [count - 1], each, shares, 0, sure, at, size)
        diagonal[at] = swap(piece, count - 1)
        after = lax.optimization_barrier((slots, piece))[0]
    near = range(1, count - 1)
    *pieces, own, sums = gather(
        after, counts, x, [*near, 0], each, shares, 0, sure, 0, heads, True
    )
    sent = [swap(piece, i + 1) for i, piece in enumerate(pieces)]
    totals = lax.psum(sums, "space")
    factors = lax.rsqrt(totals / CHANNELS + EPSILON)

    groups = []
    for at, size in ranges:
        outs = spatial(slots, counts, x, factors, *gains, at, size, count, each, shares)
        groups.append((at, list(outs)))
    last = groups[-1][1][0]

    crowd = jnp.sum((frame_count.reshape(shares, width) >= 2).astype(jnp.float32), axis=1)
    crowd = jnp.max(crowd)
    early = diagonal[ranges[-1][0]]
    *sent, last = lax.optimization_barrier((*sent, *diagonal.values(), last))
    diagonal = dict(zip(diagonal, sent[len(near) :]))
    ready = sent
    far = {}
    for at, size in ranges:
        far[at] = [(pair, place, at) for pair in (own, *sent[: len(near)]) for place in range(2)]
        far[at] += [(diagonal[at], place, 0) for place in range(2)]
    mine = position_factors([(far[at], size) for at, size in ranges])
    weights = {
        at: [
            (
                temporal_weights(
                    slots, counts, mine, far[at], *gains, each, shares, 0, part, at, size
                ),
                at,
            )
        ]
        for at, size in ranges
    }
    p = weights[0][0][0]
    if sure < block:

        def exchanged():
            spare = gather(
                slots, counts, x, range(count), each, shares, sure, block - sure, 0, heads
            )
            spare = lax.all_to_all(jnp.stack(spare)[slots], "tm", 0, 0)[slots]
            spare = [(spare[slot], place, 0) for slot in range(count) for place in range(2)]
            scale = position_factors([(spare, heads)])
            return temporal_weights(
                slots, counts, scale, spare, *gains, each, shares, sure, part, 0, heads
            )

        def single():
            wide = count * part
            row = lax.broadcasted_iota(jnp.int32, (wide, wide), 0)
            column = lax.broadcasted_iota(jnp.int32, (wide, wide), 1)
            hit = ((row - column) % part == 0) & (column // part == me)
            return jnp.broadcast_to(
                hit.astype(jnp.bfloat16), (heads, (block - sure) // part, wide, wide)
            )

        others = lax.cond(crowd > float(sure * each), exchanged, single)
        for at, _ in ranges:
            weights[at].append((others, 0))

    scales = jnp.transpose(step_scale[timestep[slots]], (1, 0, 2))
    weight = head_weight[:, None, :]
    sends = [(outs, offset) for _, outs in groups for offset in range(1, count)]
    for i, (outs, offset) in enumerate(sends):
        after = (early,) if i < 2 else ready if i < 5 else (p,)
        outs[offset] = lax.optimization_barrier((outs[offset], *after))[0]

    core = lax.axis_index("space")
    rounds = [(r, u) for r in range(each) for u in range(shares)]
    frames = [(core - u) % shares * each + (me - r) % each for r, u in rounds]
    order = jnp.concatenate([slots, me ^ jnp.stack(frames)])
    total = []
    for at, outs in groups:
        mixed = [outs[0]] + [swap(outs[offset], offset) for offset in range(1, count)]
        total = mix(
            order, counts, weights[at], scales, weight, total, mixed, at, each, shares, part
        )
    logits = jnp.zeros((width,), jnp.float32)
    for r in range(each):
        sums = jnp.zeros((2, width), jnp.float32)
        for u in range(shares):
            pairs = [
                (
                    (s * each + (f + r) % each) * shares + (f // each + u) % shares,
                    f * shares + s,
                )
                for f in range(count)
                for s in range(shares)
            ]
            sums = sums + lax.ppermute(total[r * shares + u], ("tm", "space"), pairs)
        logits = logits + sums[0] * lax.rsqrt(sums[1] / CHANNELS + EPSILON)
    return logits[None, :]


def solution(mesh):
    in_specs = (
        P(("dp", "tm"), None, None, "space", None),
        P("space", None),
        P("space", None),
        P("space", None),
        P(None, "space", None),
        P("dp"),
        P("dp"),
    )
    return jax.shard_map(
        functools.partial(on_device, count=mesh.shape["tm"], shares=mesh.shape["space"]),
        mesh=mesh,
        in_specs=in_specs,
        out_specs=P(("dp", "tm"), "space"),
        check_vma=False,
    )
```

```python
import functools

import jax
import jax.numpy as jnp
from jax import lax
from jax.experimental import pallas as pl
from jax.experimental.pallas import tpu as pltpu
from jax.sharding import PartitionSpec as P

HEADS = 40
HEAD = 128
CHANNELS = HEADS * HEAD
EPSILON = 1e-06
LOG2E = 1.4426950408889634
SCALE2 = HEAD ** (-0.5) * LOG2E
MASKED = -1e30
NT = (((1,), (1,)), ((), ()))
VMEM_LIMIT = 48 * 1024 * 1024


def lane_sums(acc):
    pieces = []
    for start in range(0, acc.shape[0], HEAD):
        pieces.append(jnp.sum(acc[start : start + HEAD].T, axis=0, keepdims=True))
    return jnp.concatenate(pieces, axis=1)


def spread_rows(row):
    pieces = []
    for start in range(0, row.shape[1], HEAD):
        piece = jnp.broadcast_to(row[:, start : start + HEAD], (HEAD, HEAD))
        pieces.append(piece.T)
    return jnp.concatenate(pieces, axis=0)


def store_shares(count_ref, rank_ref, frames_ref=None):
    shares, width = rank_ref.shape
    lines = width // HEAD
    many = jnp.where(count_ref[...] >= 2, 1.0, 0.0)
    row = lax.broadcasted_iota(jnp.int32, (HEAD, HEAD), 0)
    column = lax.broadcasted_iota(jnp.int32, (HEAD, HEAD), 1)
    upto = jnp.dot(
        many, jnp.where(row <= column, 1.0, 0.0), preferred_element_type=jnp.float32
    )
    lane = lax.broadcasted_iota(jnp.int32, (1, HEAD), 1).astype(jnp.float32)
    for share in range(shares):
        total = jnp.zeros((1, 1), jnp.float32)
        before = []
        for line in range(share * lines, (share + 1) * lines):
            before.append(upto[line : line + 1] - many[line : line + 1] + total)
            total = total + upto[line : line + 1, HEAD - 1 :]
        for i in range(lines):
            line = share * lines + i
            later = total + (lane + float(i * HEAD)) - before[i]
            rank = jnp.where(many[line : line + 1] > 0.5, before[i], later)
            here = (slice(share, share + 1), slice(i * HEAD, (i + 1) * HEAD))
            rank_ref[here] = rank.astype(jnp.int32)
            if frames_ref is not None:
                frames_ref[here] = count_ref[line : line + 1].astype(jnp.float32)


def picks(rank_ref, owner, each, first, size):
    width = rank_ref.shape[1]
    place = lax.broadcasted_iota(jnp.int32, (size, width), 0) + first
    return rank_ref[pl.ds(lax.div(owner, each), 1), :] == place * each + lax.rem(owner, each)


def gather_kernel(slots_ref, count_ref, *refs, offsets, each, first, with_sums):
    number = len(offsets)
    sources = 2 if with_sums else 2 * number
    sources, refs = refs[:sources], refs[sources:]
    outs, refs = refs[:number], refs[number:]
    if with_sums:
        out_ref, rank_ref, pick_ref, acc_ref = refs
    else:
        rank_ref, pick_ref = refs
    step = pl.program_id(0)
    size = outs[0].shape[2]

    @pl.when(step == 0)
    def _():
        store_shares(count_ref, rank_ref)
        for i, offset in enumerate(offsets):
            hit = picks(rank_ref, slots_ref[offset], each, first, size)
            pick_ref[i] = jnp.where(hit, 1.0, 0.0).astype(jnp.bfloat16)
        if with_sums:
            acc_ref[...] = jnp.zeros_like(acc_ref)

    width = rank_ref.shape[1]
    for i, offset in enumerate(offsets):
        start = pl.multiple_of(lax.div(slots_ref[offset], each) * width, width)
        for h in range(outs[i].shape[1]):
            if with_sums:
                rows = [source[0, h, pl.ds(start, width), :] for source in sources]
            else:
                rows = [source[0, h] for source in sources[2 * i : 2 * i + 2]]
            rows = jnp.concatenate(rows, axis=1)
            rows = jnp.dot(pick_ref[i], rows, preferred_element_type=jnp.float32)
            rows = rows.astype(jnp.bfloat16)
            outs[i][0, h] = rows[:, :HEAD]
            outs[i][1, h] = rows[:, HEAD:]
    if with_sums:
        for which in range(2):
            sums = acc_ref[which]
            for h in range(sources[which].shape[1]):
                wide = sources[which][0, h].astype(jnp.float32)
                sums = sums + wide * wide
            acc_ref[which] = sums

        @pl.when(step == pl.num_programs(0) - 1)
        def _():
            for which in range(2):
                out_ref[which : which + 1] = lane_sums(acc_ref[which])


def gather(slots, counts, x, offsets, each, shares, first, size, at, heads, with_sums=False):
    pixels = x.shape[2]
    step = max(i for i in range(1, 6) if heads % i == 0 and at % i == 0)
    step = step // 2 if step == heads and step % 2 == 0 else step
    skip = at // step
    width = pixels // shares

    def source(which, offset):
        return pl.BlockSpec(
            (1, step, width, HEAD), lambda h, s: (which, skip + h, lax.div(s[offset], each), 0)
        )

    in_specs = [pl.BlockSpec(counts.shape, lambda h, s: (0, 0))]
    if not with_sums:
        in_specs += [source(which, offset) for offset in offsets for which in range(2)]
    out_specs = [pl.BlockSpec((2, step, size, HEAD), lambda h, s: (0, h, 0, 0))] * len(offsets)
    out_shape = [jax.ShapeDtypeStruct((2, heads, size, HEAD), jnp.bfloat16)] * len(offsets)
    scratch = [
        pltpu.VMEM((shares, width), jnp.int32),
        pltpu.VMEM((len(offsets), size, width), jnp.bfloat16),
    ]
    if with_sums:
        for which in range(2):
            in_specs.append(
                pl.BlockSpec(
                    (1, step, pixels, HEAD), lambda h, s, which=which: (which, skip + h, 0, 0)
                )
            )
        out_specs.append(pl.BlockSpec((2, pixels), lambda h, s: (0, 0)))
        out_shape.append(jax.ShapeDtypeStruct((2, pixels), jnp.float32))
        scratch.append(pltpu.VMEM((2, pixels, HEAD), jnp.float32))
    return pl.pallas_call(
        functools.partial(
            gather_kernel, offsets=tuple(offsets), each=each, first=first, with_sums=with_sums
        ),
        grid_spec=pltpu.PrefetchScalarGridSpec(
            num_scalar_prefetch=1,
            grid=(heads // step,),
            in_specs=in_specs,
            out_specs=out_specs,
            scratch_shapes=scratch,
        ),
        out_shape=out_shape,
        compiler_params=pltpu.CompilerParams(vmem_limit_bytes=VMEM_LIMIT),
        cost_estimate=pl.CostEstimate(
            flops=4 * heads * pixels * HEAD,
            bytes_accessed=4 * heads * (len(offsets) * size + pixels) * HEAD,
            transcendentals=0,
        ),
        name="gather_sums" if with_sums else "gather",
    )(slots, counts, *[x] * (len(in_specs) - 1))


def first_kernel(slots_ref, count_ref, x_ref, out_ref, rank_ref, held_ref, sems, *, offset, each, at):
    width = held_ref.shape[2]
    owner = slots_ref[offset]
    start = pl.multiple_of(lax.div(owner, each) * width, width)
    copies = [
        [
            pltpu.make_async_copy(
                x_ref.at[which, at + h, pl.ds(start, width)],
                held_ref.at[which, h],
                sems.at[which, h],
            )
            for which in range(2)
        ]
        for h in range(held_ref.shape[1])
    ]
    for pair in copies:
        for copy in pair:
            copy.start()
    store_shares(count_ref, rank_ref)
    hit = picks(rank_ref, owner, each, 0, out_ref.shape[2])
    hit = jnp.where(hit, 1.0, 0.0).astype(jnp.bfloat16)
    for h, pair in enumerate(copies):
        for copy in pair:
            copy.wait()
        rows = jnp.concatenate([held_ref[0, h], held_ref[1, h]], axis=1)
        rows = jnp.dot(hit, rows, preferred_element_type=jnp.float32).astype(jnp.bfloat16)
        out_ref[0, h] = rows[:, :HEAD]
        out_ref[1, h] = rows[:, HEAD:]


def gather_first(slots, counts, x, offset, each, shares, size, at, heads):
    pixels = x.shape[2]
    width = pixels // shares
    return pl.pallas_call(
        functools.partial(first_kernel, offset=offset, each=each, at=at),
        grid_spec=pltpu.PrefetchScalarGridSpec(
            num_scalar_prefetch=1,
            grid=(1,),
            in_specs=[
                pl.BlockSpec(counts.shape, lambda h, s: (0, 0)),
                pl.BlockSpec(memory_space=pl.ANY),
            ],
            out_specs=[
                pl.BlockSpec((2, heads, size, HEAD), lambda h, s: (0, 0, 0, 0)),
                pl.BlockSpec((shares, width), lambda h, s: (0, 0)),
            ],
            scratch_shapes=[
                pltpu.VMEM((2, heads, width, HEAD), jnp.bfloat16),
                pltpu.SemaphoreType.DMA((2, heads)),
            ],
        ),
        out_shape=[
            jax.ShapeDtypeStruct((2, heads, size, HEAD), jnp.bfloat16),
            jax.ShapeDtypeStruct((shares, width), jnp.int32),
        ],
        compiler_params=pltpu.CompilerParams(vmem_limit_bytes=VMEM_LIMIT),
        cost_estimate=pl.CostEstimate(
            flops=4 * heads * pixels * HEAD,
            bytes_accessed=4 * heads * (size + pixels) * HEAD,
            transcendentals=0,
        ),
        name="gather_first",
    )(slots, counts, x)


def spatial_kernel(
    slots_ref, count_ref, q_ref, k_ref, v_ref, factor_ref, qg_ref, kg_ref, *rest, count, each
):
    outs, rest = rest[:count], rest[count:]
    fq_ref, fk_ref, qn_ref, kn_ref, ve_ref, rank_ref, pick_ref = rest
    width = rank_ref.shape[1]

    @pl.when(pl.program_id(0) == 0)
    def _():
        fq_ref[...] = spread_rows(factor_ref[0:1])
        fk_ref[...] = spread_rows(factor_ref[1:2])
        ve_ref[:, :, HEAD:] = jnp.ones((ve_ref.shape[0], ve_ref.shape[1], HEAD), jnp.bfloat16)
        store_shares(count_ref, rank_ref)
        for slot in range(count):
            hit = picks(rank_ref, slots_ref[slot], each, 0, pick_ref.shape[1])
            pick_ref[slot] = jnp.where(hit, 1.0, 0.0).astype(jnp.bfloat16)

    many = q_ref.shape[1]
    for h in range(many):
        qn = q_ref[0, h].astype(jnp.float32) * fq_ref[...] * qg_ref[h]
        qn_ref[:, h * HEAD : (h + 1) * HEAD] = qn.astype(jnp.bfloat16)
        kn = k_ref[0, h].astype(jnp.float32) * fk_ref[...] * kg_ref[h]
        kn_ref[h] = kn.astype(jnp.bfloat16)
        ve_ref[h, :, :HEAD] = v_ref[0, h]
    for slot in range(count):
        start = pl.multiple_of(lax.div(slots_ref[slot], each) * width, width)
        picked = jnp.dot(
            pick_ref[slot], qn_ref[pl.ds(start, width), :], preferred_element_type=jnp.float32
        ).astype(jnp.bfloat16)
        for h in range(many):
            qn = picked[:, h * HEAD : (h + 1) * HEAD]
            s = lax.dot_general(qn, kn_ref[h], NT, preferred_element_type=jnp.float32)
            top = jnp.max(s, axis=1, keepdims=True)
            p = jnp.exp2(s * SCALE2 - top * SCALE2).astype(jnp.bfloat16)
            o = jnp.dot(p, ve_ref[h], preferred_element_type=jnp.float32)
            outs[slot][h] = (o[:, :HEAD] / o[:, HEAD:]).astype(jnp.bfloat16)


def spatial(slots, counts, x, factors, q_gain, k_gain, first, size, count, each, shares):
    pixels = x.shape[2]
    block, width = pixels // count, pixels // shares

    def rows(which):
        return pl.BlockSpec((1, step, pixels, HEAD), lambda h, s: (which, skip + h, 0, 0))

    step = 2 if size % 2 == 0 and first % 2 == 0 else 1
    skip = first // step
    gain = pl.BlockSpec((step, 1, HEAD), lambda h, s: (skip + h, 0, 0))
    return pl.pallas_call(
        functools.partial(spatial_kernel, count=count, each=each),
        grid_spec=pltpu.PrefetchScalarGridSpec(
            num_scalar_prefetch=1,
            grid=(size // step,),
            in_specs=[
                pl.BlockSpec(counts.shape, lambda h, s: (0, 0)),
                rows(0),
                rows(1),
                rows(2),
                pl.BlockSpec((2, pixels), lambda h, s: (0, 0)),
                gain,
                gain,
            ],
            out_specs=[pl.BlockSpec((step, block, HEAD), lambda h, s: (h, 0, 0))] * count,
            scratch_shapes=[
                pltpu.VMEM((pixels, HEAD), jnp.float32),
                pltpu.VMEM((pixels, HEAD), jnp.float32),
                pltpu.VMEM((pixels, step * HEAD), jnp.bfloat16),
                pltpu.VMEM((step, pixels, HEAD), jnp.bfloat16),
                pltpu.VMEM((step, pixels, 2 * HEAD), jnp.bfloat16),
                pltpu.VMEM((shares, width), jnp.int32),
                pltpu.VMEM((count, block, width), jnp.bfloat16),
            ],
        ),
        out_shape=[jax.ShapeDtypeStruct((size, block, HEAD), jnp.bfloat16)] * count,
        compiler_params=pltpu.CompilerParams(vmem_limit_bytes=VMEM_LIMIT),
        cost_estimate=pl.CostEstimate(
            flops=8 * size * pixels * pixels * HEAD,
            bytes_accessed=8 * size * pixels * HEAD,
            transcendentals=size * pixels * pixels,
        ),
        name="spatial_attention",
    )(slots, counts, x, x, x, factors, q_gain, k_gain)


def far_sums_kernel(*refs):
    far, (out_ref, acc_ref) = refs[:-2], refs[-2:]
    head = pl.program_id(0)
    block = far[0].shape[2]

    @pl.when(head == 0)
    def _():
        acc_ref[...] = jnp.zeros_like(acc_ref)

    for i, ref in enumerate(far):
        which, at = i % 2, i // 2 * block
        sums = acc_ref[which, at : at + block]
        for h in range(ref.shape[1]):
            wide = ref[0, h].astype(jnp.float32)
            sums = sums + wide * wide
        acc_ref[which, at : at + block] = sums

    @pl.when(head == pl.num_programs(0) - 1)
    def _():
        for which in range(2):
            out_ref[which : which + 1] = lane_sums(acc_ref[which])


def far_sums(far, heads):
    block = far[0][0].shape[2]
    rows = len(far) // 2 * block
    step = max(i for i in range(1, 6) if all(n % i == 0 for n in (heads, *[f[2] for f in far])))
    return pl.pallas_call(
        far_sums_kernel,
        grid=(heads // step,),
        in_specs=[
            pl.BlockSpec(
                (1, step, block, HEAD),
                lambda h, place=place, skip=at // step: (place, skip + h, 0, 0),
            )
            for _, place, at in far
        ],
        out_specs=pl.BlockSpec((2, rows), lambda h: (0, 0)),
        out_shape=jax.ShapeDtypeStruct((2, rows), jnp.float32),
        scratch_shapes=[pltpu.VMEM((2, rows, HEAD), jnp.float32)],
        compiler_params=pltpu.CompilerParams(vmem_limit_bytes=VMEM_LIMIT),
        cost_estimate=pl.CostEstimate(
            flops=4 * heads * rows * HEAD, bytes_accessed=4 * heads * rows * HEAD, transcendentals=0
        ),
        name="far_sums",
    )(*[array for array, _, _ in far])


def weights_kernel(
    slots_ref, count_ref, factor_ref, frame_ref, qg_ref, kg_ref, *rest, each, first, part
):
    far, rest = rest[:-7], rest[-7:]
    out_ref, fq_ref, fk_ref, rank_ref, frames_ref, bias_ref, unit_ref = rest
    count = len(far) // 2
    size = far[0].shape[2]
    wide = count * part

    @pl.when(pl.program_id(0) == 0)
    def _():
        fq_ref[...] = spread_rows(factor_ref[0:1])
        fk_ref[...] = spread_rows(factor_ref[1:2])
        store_shares(count_ref, rank_ref, frames_ref)
        me = slots_ref[0]
        frames = frames_ref[pl.ds(lax.div(me, each), 1), :]
        hit = picks(rank_ref, me, each, first, size)
        frames = jnp.sum(jnp.where(hit, frames, 0.0), axis=1, keepdims=True)
        row = lax.broadcasted_iota(jnp.int32, (wide, 2 * wide), 0)
        column = lax.broadcasted_iota(jnp.int32, (wide, 2 * wide), 1)
        same = (((row - column) & (part - 1)) == 0) & (column < wide)
        unit_ref[...] = jnp.where(column - row == wide, 1.0, 0.0)
        for j in range(size // part):
            held = jnp.concatenate([frames[j * part : (j + 1) * part]] * count, axis=0)
            live = jnp.where(frame_ref[...] < held, 0.0, MASKED)
            bias_ref[j] = jnp.where(same, live, MASKED)

    def normal(which, factor, gain, at):
        pieces = []
        for slot in range(count):
            rows = far[2 * slot + which][0, 0, at : at + part].astype(jnp.float32)
            rows = rows * factor[slot * size + at : slot * size + at + part] * gain
            pieces.append(rows.astype(jnp.bfloat16))
        return jnp.concatenate(pieces, axis=0)

    for j in range(size // part):
        qn = normal(0, fq_ref, qg_ref[0], j * part)
        kn = normal(1, fk_ref, kg_ref[0], j * part)
        kn = jnp.concatenate([kn, kn], axis=0)
        s = lax.dot_general(qn, kn, NT, preferred_element_type=jnp.float32) * SCALE2 + bias_ref[j]
        e = jnp.exp2(s - jnp.max(s, axis=1, keepdims=True))
        p = e * (1.0 / jnp.sum(e, axis=1, keepdims=True)) + unit_ref[...]
        out_ref[0, j] = p.astype(jnp.bfloat16)


def position_factors(parts):
    sums = functools.reduce(jnp.add, [far_sums(far, heads) for far, heads in parts])
    factors = lax.rsqrt(lax.psum(sums, "space") / CHANNELS + EPSILON)
    return jnp.pad(factors, ((0, 0), (0, -factors.shape[1] % HEAD)))


def temporal_weights(
    slots, counts, factors, far, q_gain, k_gain, each, shares, first, part, start, heads
):
    count = len(far) // 2
    size = far[0][0].shape[2]
    rows, wide, subs = count * size, count * part, size // part
    width = counts.size // shares
    padded = factors.shape[1]
    frame = jnp.tile(jnp.repeat(slots, part), 2)[None, :].astype(jnp.float32)
    gain = pl.BlockSpec((1, 1, HEAD), lambda h, s: (start + h, 0, 0))
    return pl.pallas_call(
        functools.partial(weights_kernel, each=each, first=first, part=part),
        grid_spec=pltpu.PrefetchScalarGridSpec(
            num_scalar_prefetch=1,
            grid=(heads,),
            in_specs=[
                pl.BlockSpec(counts.shape, lambda h, s: (0, 0)),
                pl.BlockSpec((2, padded), lambda h, s: (0, 0)),
                pl.BlockSpec((1, 2 * wide), lambda h, s: (0, 0)),
                gain,
                gain,
            ]
            + [
                pl.BlockSpec(
                    (1, 1, size, HEAD), lambda h, s, place=place, at=at: (place, at + h, 0, 0)
                )
                for _, place, at in far
            ],
            out_specs=pl.BlockSpec((1, subs, wide, 2 * wide), lambda h, s: (h, 0, 0, 0)),
            scratch_shapes=[
                pltpu.VMEM((padded, HEAD), jnp.float32),
                pltpu.VMEM((padded, HEAD), jnp.float32),
                pltpu.VMEM((shares, width), jnp.int32),
                pltpu.VMEM((shares, width), jnp.float32),
                pltpu.VMEM((subs, wide, 2 * wide), jnp.float32),
                pltpu.VMEM((wide, 2 * wide), jnp.float32),
            ],
        ),
        out_shape=jax.ShapeDtypeStruct((heads, subs, wide, 2 * wide), jnp.bfloat16),
        compiler_params=pltpu.CompilerParams(vmem_limit_bytes=VMEM_LIMIT),
        cost_estimate=pl.CostEstimate(
            flops=2 * heads * rows * wide * HEAD,
            bytes_accessed=4 * heads * rows * HEAD + 2 * heads * rows * wide,
            transcendentals=heads * rows * wide,
        ),
        name="temporal_weights",
    )(slots, counts, factors, frame, q_gain, k_gain, *[array for array, _, _ in far])


def mix_kernel(
    slots_ref, rank_ref, scale_ref, weight_ref, *rest, count, each, shares, part, more, single
):
    mixed, rest = rest[:count], rest[count:]
    weights, rest = rest[: -(2 + (1 + more) * shares)], rest[-(2 + (1 + more) * shares) :]
    before, outs, (dot_ref, square_ref) = rest[: more * shares], rest[more * shares : -2], rest[-2:]
    head = pl.program_id(0)
    block = mixed[0].shape[1]

    if not single:

        @pl.when(head == 0)
        def _():
            dot_ref[...] = jnp.zeros_like(dot_ref)
            square_ref[...] = jnp.zeros_like(square_ref)

    subs = [(ref, j) for ref in weights for j in range(ref.shape[1])]
    for sub, (p_ref, j) in enumerate(subs):
        at = sub * part
        if single:
            dots = [jnp.zeros((part, HEAD), jnp.float32)] * count
            squares = list(dots)
        else:
            dots = [dot_ref[slot, at : at + part] for slot in range(count)]
            squares = [square_ref[slot, at : at + part] for slot in range(count)]
        for h in range(p_ref.shape[0]):
            o = jnp.concatenate([mixed[slot][h, at : at + part] for slot in range(count)], axis=0)
            o = jnp.concatenate([o, o], axis=0)
            both = jnp.dot(p_ref[h, j], o, preferred_element_type=jnp.float32)
            for slot in range(count):
                m = both[slot * part : (slot + 1) * part] * scale_ref[h, slot : slot + 1]
                dots[slot] = dots[slot] + m * weight_ref[h]
                squares[slot] = squares[slot] + m * m
        for slot in range(count):
            dot_ref[slot, at : at + part] = dots[slot]
            square_ref[slot, at : at + part] = squares[slot]

    @pl.when(head == pl.num_programs(0) - 1)
    def _():
        hit = picks(rank_ref, slots_ref[0], each, 0, block)
        for i in range(count):
            share, r = i // each, i % each
            for which, ref in enumerate((dot_ref, square_ref)):
                sums = jnp.sum(ref[slots_ref[count + i]], axis=1, keepdims=True)
                sums = jnp.sum(jnp.where(hit, sums, 0.0), axis=0, keepdims=True)
                if more:
                    sums = before[share][r, which : which + 1] + sums
                outs[share][r, which : which + 1] = sums


def mix(slots, ranks, weights, scales, weight, before, mixed, first, each, shares, part):
    count = len(mixed)
    size, block, _ = mixed[0].shape
    wide = count * part
    rows = count * block
    width = ranks.shape[1]
    step = max(i for i in range(1, 6) if size % i == 0 and first % i == 0)
    skip = first // step
    out = pl.BlockSpec((each, 2, width), lambda h, s: (0, 0, 0))
    return pl.pallas_call(
        functools.partial(
            mix_kernel,
            count=count,
            each=each,
            shares=shares,
            part=part,
            more=len(before) // shares,
            single=size == step,
        ),
        grid_spec=pltpu.PrefetchScalarGridSpec(
            num_scalar_prefetch=1,
            grid=(size // step,),
            in_specs=[
                pl.BlockSpec(ranks.shape, lambda h, s: (0, 0)),
                pl.BlockSpec((step, count, HEAD), lambda h, s: (skip + h, 0, 0)),
                pl.BlockSpec((step, 1, HEAD), lambda h, s: (skip + h, 0, 0)),
            ]
            + [pl.BlockSpec((step, block, HEAD), lambda h, s: (h, 0, 0))] * count
            + [
                pl.BlockSpec(
                    (step, *p.shape[1:]),
                    lambda h, s, skip=(first - at) // step: (skip + h, 0, 0, 0),
                )
                for p, at in weights
            ]
            + [out] * len(before),
            out_specs=[out] * shares,
            scratch_shapes=[
                pltpu.VMEM((count, block, HEAD), jnp.float32),
                pltpu.VMEM((count, block, HEAD), jnp.float32),
            ],
        ),
        out_shape=[jax.ShapeDtypeStruct((each, 2, width), jnp.float32)] * shares,
        compiler_params=pltpu.CompilerParams(vmem_limit_bytes=VMEM_LIMIT),
        cost_estimate=pl.CostEstimate(
            flops=2 * size * rows * wide * HEAD,
            bytes_accessed=2 * size * rows * (HEAD + wide),
            transcendentals=0,
        ),
        name="temporal_mix",
    )(slots, ranks, scales, weight, *mixed, *[p for p, _ in weights], *before)


def on_device(
    projected, q_gain, k_gain, head_weight, step_scale, timestep, frame_count, *, count, shares
):
    x = jnp.transpose(projected[0], (1, 2, 0, 3))
    heads, pixels = x.shape[1], x.shape[2]
    block, width, each = pixels // count, pixels // shares, count // shares
    part = 16
    sure = min(block, -(-13 * block // (16 * part)) * part)
    me = lax.axis_index("tm")
    slots = me ^ jnp.arange(count, dtype=jnp.int32)
    counts = frame_count.reshape(pixels // HEAD, HEAD)
    gains = (q_gain[:, None, :], k_gain[:, None, :])

    def swap(value, offset):
        return lax.ppermute(value, "tm", [(i, i ^ offset) for i in range(count)])

    first = heads * 4 // 5 if heads % 20 == 0 else heads
    ranges = [(at, size) for at, size in ((0, first), (first, heads - first)) if size]
    diagonal = {}
    after = slots
    for at, size in reversed(ranges):
        if after is slots:
            piece, ranks = gather_first(
                after, counts, x, count - 1, each, shares, sure, at, size
            )
        else:
            (piece,) = gather(after, counts, x, [count - 1], each, shares, 0, sure, at, size)
        diagonal[at] = swap(piece, count - 1)
        after = lax.optimization_barrier((slots, piece))[0]
    near = range(1, count - 1)
    *pieces, own, sums = gather(
        after, counts, x, [*near, 0], each, shares, 0, sure, 0, heads, True
    )
    sent = [swap(piece, i + 1) for i, piece in enumerate(pieces)]
    totals = lax.psum(sums, "space")
    factors = lax.rsqrt(totals / CHANNELS + EPSILON)

    groups = []
    for at, size in ranges:
        outs = spatial(slots, counts, x, factors, *gains, at, size, count, each, shares)
        groups.append((at, list(outs)))
    last = groups[-1][1][0]

    crowd = jnp.sum((frame_count.reshape(shares, width) >= 2).astype(jnp.float32), axis=1)
    crowd = jnp.max(crowd)
    early = diagonal[ranges[-1][0]]
    *sent, last = lax.optimization_barrier((*sent, *diagonal.values(), last))
    diagonal = dict(zip(diagonal, sent[len(near) :]))
    ready = sent
    far = {}
    for at, size in ranges:
        far[at] = [(pair, place, at) for pair in (own, *sent[: len(near)]) for place in range(2)]
        far[at] += [(diagonal[at], place, 0) for place in range(2)]
    mine = position_factors([(far[at], size) for at, size in ranges])
    weights = {
        at: [
            (
                temporal_weights(
                    slots, counts, mine, far[at], *gains, each, shares, 0, part, at, size
                ),
                at,
            )
        ]
        for at, size in ranges
    }
    p = weights[0][0][0]
    if sure < block:

        def exchanged():
            spare = gather(
                slots, counts, x, range(count), each, shares, sure, block - sure, 0, heads
            )
            spare = lax.all_to_all(jnp.stack(spare)[slots], "tm", 0, 0)[slots]
            spare = [(spare[slot], place, 0) for slot in range(count) for place in range(2)]
            scale = position_factors([(spare, heads)])
            return temporal_weights(
                slots, counts, scale, spare, *gains, each, shares, sure, part, 0, heads
            )

        def single():
            wide = count * part
            row = lax.broadcasted_iota(jnp.int32, (wide, 2 * wide), 0)
            column = lax.broadcasted_iota(jnp.int32, (wide, 2 * wide), 1)
            hit = ((row - column) % part == 0) & (column // part == me)
            hit = hit | (column - row == wide)
            return jnp.broadcast_to(
                hit.astype(jnp.bfloat16), (heads, (block - sure) // part, wide, 2 * wide)
            )

        others = lax.cond(crowd > float(sure * each), exchanged, single)
        for at, _ in ranges:
            weights[at].append((others, 0))

    scales = jnp.transpose(step_scale[timestep[slots]], (1, 0, 2))
    weight = head_weight[:, None, :]
    sends = [(outs, offset) for _, outs in groups for offset in range(1, count)]
    for i, (outs, offset) in enumerate(sends):
        after = (early,) if i < 2 else ready if i < 5 else (p,)
        outs[offset] = lax.optimization_barrier((outs[offset], *after))[0]

    core = lax.axis_index("space")
    frames = [
        (core - u) % shares * each + (me - r) % each for u in range(shares) for r in range(each)
    ]
    order = jnp.concatenate([slots, me ^ jnp.stack(frames)])
    total = []
    for at, outs in groups:
        mixed = [outs[0]] + [swap(outs[offset], offset) for offset in range(1, count)]
        total = mix(
            order, ranks, weights[at], scales, weight, total, mixed, at, each, shares, part
        )
    sums = total[0]
    for u in range(1, shares):
        turn = [(c, (c - u) % shares) for c in range(shares)]
        sums = sums + lax.ppermute(total[u], "space", turn)
    logits = sums[:, 0] * lax.rsqrt(sums[:, 1] / CHANNELS + EPSILON)
    mine = jnp.zeros((width,), jnp.float32)
    for r in range(each):
        pairs = [
            ((s * each + (f + r) % each) * shares + f // each, f * shares + s)
            for f in range(count)
            for s in range(shares)
        ]
        mine = mine + lax.ppermute(logits[r], ("tm", "space"), pairs)
    return mine[None, :]


def solution(mesh):
    in_specs = (
        P(("dp", "tm"), None, None, "space", None),
        P("space", None),
        P("space", None),
        P("space", None),
        P(None, "space", None),
        P("dp"),
        P("dp"),
    )
    return jax.shard_map(
        functools.partial(on_device, count=mesh.shape["tm"], shares=mesh.shape["space"]),
        mesh=mesh,
        in_specs=in_specs,
        out_specs=P(("dp", "tm"), "space"),
        check_vma=False,
    )
```

```python
import functools

import jax
import jax.numpy as jnp
from jax import lax
from jax.experimental import pallas as pl
from jax.experimental.pallas import tpu as pltpu
from jax.sharding import PartitionSpec as P

HEADS = 40
HEAD = 128
CHANNELS = HEADS * HEAD
EPSILON = 1e-06
LOG2E = 1.4426950408889634
SCALE2 = HEAD ** (-0.5) * LOG2E
MASKED = -1e30
NT = (((1,), (1,)), ((), ()))
VMEM_LIMIT = 48 * 1024 * 1024


def lane_sums(acc):
    pieces = []
    for start in range(0, acc.shape[0], HEAD):
        pieces.append(jnp.sum(acc[start : start + HEAD].T, axis=0, keepdims=True))
    return jnp.concatenate(pieces, axis=1)


def spread_rows(row):
    pieces = []
    for start in range(0, row.shape[1], HEAD):
        piece = jnp.broadcast_to(row[:, start : start + HEAD], (HEAD, HEAD))
        pieces.append(piece.T)
    return jnp.concatenate(pieces, axis=0)


def store_shares(count_ref, rank_ref, frames_ref=None):
    shares, width = rank_ref.shape
    lines = width // HEAD
    many = jnp.where(count_ref[...] >= 2, 1.0, 0.0)
    row = lax.broadcasted_iota(jnp.int32, (HEAD, HEAD), 0)
    column = lax.broadcasted_iota(jnp.int32, (HEAD, HEAD), 1)
    upto = jnp.dot(
        many, jnp.where(row <= column, 1.0, 0.0), preferred_element_type=jnp.float32
    )
    lane = lax.broadcasted_iota(jnp.int32, (1, HEAD), 1).astype(jnp.float32)
    for share in range(shares):
        total = jnp.zeros((1, 1), jnp.float32)
        before = []
        for line in range(share * lines, (share + 1) * lines):
            before.append(upto[line : line + 1] - many[line : line + 1] + total)
            total = total + upto[line : line + 1, HEAD - 1 :]
        for i in range(lines):
            line = share * lines + i
            later = total + (lane + float(i * HEAD)) - before[i]
            rank = jnp.where(many[line : line + 1] > 0.5, before[i], later)
            here = (slice(share, share + 1), slice(i * HEAD, (i + 1) * HEAD))
            rank_ref[here] = rank.astype(jnp.int32)
            if frames_ref is not None:
                frames_ref[here] = count_ref[line : line + 1].astype(jnp.float32)


def picks(rank_ref, owner, each, first, size):
    width = rank_ref.shape[1]
    place = lax.broadcasted_iota(jnp.int32, (size, width), 0) + first
    return rank_ref[pl.ds(lax.div(owner, each), 1), :] == place * each + lax.rem(owner, each)


def gather_kernel(slots_ref, count_ref, *refs, offsets, each, first, with_sums):
    number = len(offsets)
    sources = 2 if with_sums else 2 * number
    sources, refs = refs[:sources], refs[sources:]
    outs, refs = refs[:number], refs[number:]
    if with_sums:
        out_ref, rank_ref, pick_ref, acc_ref = refs
    else:
        rank_ref, pick_ref = refs
    step = pl.program_id(0)
    size = outs[0].shape[2]

    @pl.when(step == 0)
    def _():
        store_shares(count_ref, rank_ref)
        for i, offset in enumerate(offsets):
            hit = picks(rank_ref, slots_ref[offset], each, first, size)
            pick_ref[i] = jnp.where(hit, 1.0, 0.0).astype(jnp.bfloat16)
        if with_sums:
            acc_ref[...] = jnp.zeros_like(acc_ref)

    width = rank_ref.shape[1]
    for i, offset in enumerate(offsets):
        start = pl.multiple_of(lax.div(slots_ref[offset], each) * width, width)
        for h in range(outs[i].shape[1]):
            if with_sums:
                rows = [source[0, h, pl.ds(start, width), :] for source in sources]
            else:
                rows = [source[0, h] for source in sources[2 * i : 2 * i + 2]]
            rows = jnp.concatenate(rows, axis=1)
            rows = jnp.dot(pick_ref[i], rows, preferred_element_type=jnp.float32)
            rows = rows.astype(jnp.bfloat16)
            outs[i][0, h] = rows[:, :HEAD]
            outs[i][1, h] = rows[:, HEAD:]
    if with_sums:
        for which in range(2):
            sums = acc_ref[which]
            for h in range(sources[which].shape[1]):
                wide = sources[which][0, h].astype(jnp.float32)
                sums = sums + wide * wide
            acc_ref[which] = sums

        @pl.when(step == pl.num_programs(0) - 1)
        def _():
            for which in range(2):
                out_ref[which : which + 1] = lane_sums(acc_ref[which])


def gather(slots, counts, x, offsets, each, shares, first, size, at, heads, with_sums=False):
    pixels = x.shape[2]
    step = max(i for i in range(1, 6) if heads % i == 0 and at % i == 0)
    step = step // 2 if step == heads and step % 2 == 0 else step
    skip = at // step
    width = pixels // shares

    def source(which, offset):
        return pl.BlockSpec(
            (1, step, width, HEAD), lambda h, s: (which, skip + h, lax.div(s[offset], each), 0)
        )

    in_specs = [pl.BlockSpec(counts.shape, lambda h, s: (0, 0))]
    if not with_sums:
        in_specs += [source(which, offset) for offset in offsets for which in range(2)]
    out_specs = [pl.BlockSpec((2, step, size, HEAD), lambda h, s: (0, h, 0, 0))] * len(offsets)
    out_shape = [jax.ShapeDtypeStruct((2, heads, size, HEAD), jnp.bfloat16)] * len(offsets)
    scratch = [
        pltpu.VMEM((shares, width), jnp.int32),
        pltpu.VMEM((len(offsets), size, width), jnp.bfloat16),
    ]
    if with_sums:
        for which in range(2):
            in_specs.append(
                pl.BlockSpec(
                    (1, step, pixels, HEAD), lambda h, s, which=which: (which, skip + h, 0, 0)
                )
            )
        out_specs.append(pl.BlockSpec((2, pixels), lambda h, s: (0, 0)))
        out_shape.append(jax.ShapeDtypeStruct((2, pixels), jnp.float32))
        scratch.append(pltpu.VMEM((2, pixels, HEAD), jnp.float32))
    return pl.pallas_call(
        functools.partial(
            gather_kernel, offsets=tuple(offsets), each=each, first=first, with_sums=with_sums
        ),
        grid_spec=pltpu.PrefetchScalarGridSpec(
            num_scalar_prefetch=1,
            grid=(heads // step,),
            in_specs=in_specs,
            out_specs=out_specs,
            scratch_shapes=scratch,
        ),
        out_shape=out_shape,
        compiler_params=pltpu.CompilerParams(vmem_limit_bytes=VMEM_LIMIT),
        cost_estimate=pl.CostEstimate(
            flops=4 * heads * pixels * HEAD,
            bytes_accessed=4 * heads * (len(offsets) * size + pixels) * HEAD,
            transcendentals=0,
        ),
        name="gather_sums" if with_sums else "gather",
    )(slots, counts, *[x] * (len(in_specs) - 1))


def spatial_kernel(
    slots_ref, count_ref, q_ref, k_ref, v_ref, factor_ref, qg_ref, kg_ref, *rest, count, each
):
    outs, rest = rest[:count], rest[count:]
    fq_ref, fk_ref, qn_ref, kn_ref, ve_ref, rank_ref, pick_ref = rest
    width = rank_ref.shape[1]

    @pl.when(pl.program_id(0) == 0)
    def _():
        fq_ref[...] = spread_rows(factor_ref[0:1])
        fk_ref[...] = spread_rows(factor_ref[1:2])
        ve_ref[:, :, HEAD:] = jnp.ones((ve_ref.shape[0], ve_ref.shape[1], HEAD), jnp.bfloat16)
        store_shares(count_ref, rank_ref)
        for slot in range(count):
            hit = picks(rank_ref, slots_ref[slot], each, 0, pick_ref.shape[1])
            pick_ref[slot] = jnp.where(hit, 1.0, 0.0).astype(jnp.bfloat16)

    many = q_ref.shape[1]
    for h in range(many):
        qn = q_ref[0, h].astype(jnp.float32) * fq_ref[...] * qg_ref[h]
        qn_ref[:, h * HEAD : (h + 1) * HEAD] = qn.astype(jnp.bfloat16)
        kn = k_ref[0, h].astype(jnp.float32) * fk_ref[...] * kg_ref[h]
        kn_ref[h] = kn.astype(jnp.bfloat16)
        ve_ref[h, :, :HEAD] = v_ref[0, h]
    for slot in range(count):
        start = pl.multiple_of(lax.div(slots_ref[slot], each) * width, width)
        picked = jnp.dot(
            pick_ref[slot], qn_ref[pl.ds(start, width), :], preferred_element_type=jnp.float32
        ).astype(jnp.bfloat16)
        for h in range(many):
            qn = picked[:, h * HEAD : (h + 1) * HEAD]
            s = lax.dot_general(qn, kn_ref[h], NT, preferred_element_type=jnp.float32)
            top = jnp.max(s, axis=1, keepdims=True)
            p = jnp.exp2(s * SCALE2 - top * SCALE2).astype(jnp.bfloat16)
            o = jnp.dot(p, ve_ref[h], preferred_element_type=jnp.float32)
            outs[slot][h] = (o[:, :HEAD] / o[:, HEAD:]).astype(jnp.bfloat16)


def spatial(slots, counts, x, factors, q_gain, k_gain, first, size, count, each, shares):
    pixels = x.shape[2]
    block, width = pixels // count, pixels // shares

    def rows(which):
        return pl.BlockSpec((1, step, pixels, HEAD), lambda h, s: (which, skip + h, 0, 0))

    step = 2 if size % 2 == 0 and first % 2 == 0 else 1
    skip = first // step
    gain = pl.BlockSpec((step, 1, HEAD), lambda h, s: (skip + h, 0, 0))
    return pl.pallas_call(
        functools.partial(spatial_kernel, count=count, each=each),
        grid_spec=pltpu.PrefetchScalarGridSpec(
            num_scalar_prefetch=1,
            grid=(size // step,),
            in_specs=[
                pl.BlockSpec(counts.shape, lambda h, s: (0, 0)),
                rows(0),
                rows(1),
                rows(2),
                pl.BlockSpec((2, pixels), lambda h, s: (0, 0)),
                gain,
                gain,
            ],
            out_specs=[pl.BlockSpec((step, block, HEAD), lambda h, s: (h, 0, 0))] * count,
            scratch_shapes=[
                pltpu.VMEM((pixels, HEAD), jnp.float32),
                pltpu.VMEM((pixels, HEAD), jnp.float32),
                pltpu.VMEM((pixels, step * HEAD), jnp.bfloat16),
                pltpu.VMEM((step, pixels, HEAD), jnp.bfloat16),
                pltpu.VMEM((step, pixels, 2 * HEAD), jnp.bfloat16),
                pltpu.VMEM((shares, width), jnp.int32),
                pltpu.VMEM((count, block, width), jnp.bfloat16),
            ],
        ),
        out_shape=[jax.ShapeDtypeStruct((size, block, HEAD), jnp.bfloat16)] * count,
        compiler_params=pltpu.CompilerParams(vmem_limit_bytes=VMEM_LIMIT),
        cost_estimate=pl.CostEstimate(
            flops=8 * size * pixels * pixels * HEAD,
            bytes_accessed=8 * size * pixels * HEAD,
            transcendentals=size * pixels * pixels,
        ),
        name="spatial_attention",
    )(slots, counts, x, x, x, factors, q_gain, k_gain)


def far_sums_kernel(*refs):
    far, (out_ref, acc_ref) = refs[:-2], refs[-2:]
    head = pl.program_id(0)
    block = far[0].shape[2]

    @pl.when(head == 0)
    def _():
        acc_ref[...] = jnp.zeros_like(acc_ref)

    for i, ref in enumerate(far):
        which, at = i % 2, i // 2 * block
        sums = acc_ref[which, at : at + block]
        for h in range(ref.shape[1]):
            wide = ref[0, h].astype(jnp.float32)
            sums = sums + wide * wide
        acc_ref[which, at : at + block] = sums

    @pl.when(head == pl.num_programs(0) - 1)
    def _():
        for which in range(2):
            out_ref[which : which + 1] = lane_sums(acc_ref[which])


def far_sums(far, heads):
    block = far[0][0].shape[2]
    rows = len(far) // 2 * block
    step = max(i for i in range(1, 6) if all(n % i == 0 for n in (heads, *[f[2] for f in far])))
    return pl.pallas_call(
        far_sums_kernel,
        grid=(heads // step,),
        in_specs=[
            pl.BlockSpec(
                (1, step, block, HEAD),
                lambda h, place=place, skip=at // step: (place, skip + h, 0, 0),
            )
            for _, place, at in far
        ],
        out_specs=pl.BlockSpec((2, rows), lambda h: (0, 0)),
        out_shape=jax.ShapeDtypeStruct((2, rows), jnp.float32),
        scratch_shapes=[pltpu.VMEM((2, rows, HEAD), jnp.float32)],
        compiler_params=pltpu.CompilerParams(vmem_limit_bytes=VMEM_LIMIT),
        cost_estimate=pl.CostEstimate(
            flops=4 * heads * rows * HEAD, bytes_accessed=4 * heads * rows * HEAD, transcendentals=0
        ),
        name="far_sums",
    )(*[array for array, _, _ in far])


def weights_kernel(
    slots_ref, count_ref, factor_ref, frame_ref, qg_ref, kg_ref, *rest, each, first, part
):
    far, (out_ref, fq_ref, fk_ref, rank_ref, frames_ref, bias_ref) = rest[:-6], rest[-6:]
    count = len(far) // 2
    size = far[0].shape[2]
    wide = count * part

    @pl.when(pl.program_id(0) == 0)
    def _():
        fq_ref[...] = spread_rows(factor_ref[0:1])
        fk_ref[...] = spread_rows(factor_ref[1:2])
        store_shares(count_ref, rank_ref, frames_ref)
        me = slots_ref[0]
        frames = frames_ref[pl.ds(lax.div(me, each), 1), :]
        hit = picks(rank_ref, me, each, first, size)
        frames = jnp.sum(jnp.where(hit, frames, 0.0), axis=1, keepdims=True)
        row = lax.broadcasted_iota(jnp.int32, (wide, wide), 0)
        column = lax.broadcasted_iota(jnp.int32, (wide, wide), 1)
        same = ((row - column) & (part - 1)) == 0
        for j in range(size // part):
            held = jnp.concatenate([frames[j * part : (j + 1) * part]] * count, axis=0)
            live = jnp.where(frame_ref[...] < held, 0.0, MASKED)
            bias_ref[j] = jnp.where(same, live, MASKED)

    def normal(which, factor, gain, at):
        pieces = []
        for slot in range(count):
            rows = far[2 * slot + which][0, 0, at : at + part].astype(jnp.float32)
            rows = rows * factor[slot * size + at : slot * size + at + part] * gain
            pieces.append(rows.astype(jnp.bfloat16))
        return jnp.concatenate(pieces, axis=0)

    for j in range(size // part):
        qn = normal(0, fq_ref, qg_ref[0], j * part)
        kn = normal(1, fk_ref, kg_ref[0], j * part)
        s = lax.dot_general(qn, kn, NT, preferred_element_type=jnp.float32) * SCALE2 + bias_ref[j]
        e = jnp.exp2(s - jnp.max(s, axis=1, keepdims=True))
        out_ref[0, j] = (e * (1.0 / jnp.sum(e, axis=1, keepdims=True))).astype(jnp.bfloat16)


def position_factors(parts):
    sums = functools.reduce(jnp.add, [far_sums(far, heads) for far, heads in parts])
    factors = lax.rsqrt(lax.psum(sums, "space") / CHANNELS + EPSILON)
    return jnp.pad(factors, ((0, 0), (0, -factors.shape[1] % HEAD)))


def temporal_weights(
    slots, counts, factors, far, q_gain, k_gain, each, shares, first, part, start, heads
):
    count = len(far) // 2
    size = far[0][0].shape[2]
    rows, wide, subs = count * size, count * part, size // part
    width = counts.size // shares
    padded = factors.shape[1]
    frame = jnp.repeat(slots, part)[None, :].astype(jnp.float32)
    gain = pl.BlockSpec((1, 1, HEAD), lambda h, s: (start + h, 0, 0))
    return pl.pallas_call(
        functools.partial(weights_kernel, each=each, first=first, part=part),
        grid_spec=pltpu.PrefetchScalarGridSpec(
            num_scalar_prefetch=1,
            grid=(heads,),
            in_specs=[
                pl.BlockSpec(counts.shape, lambda h, s: (0, 0)),
                pl.BlockSpec((2, padded), lambda h, s: (0, 0)),
                pl.BlockSpec((1, wide), lambda h, s: (0, 0)),
                gain,
                gain,
            ]
            + [
                pl.BlockSpec(
                    (1, 1, size, HEAD), lambda h, s, place=place, at=at: (place, at + h, 0, 0)
                )
                for _, place, at in far
            ],
            out_specs=pl.BlockSpec((1, subs, wide, wide), lambda h, s: (h, 0, 0, 0)),
            scratch_shapes=[
                pltpu.VMEM((padded, HEAD), jnp.float32),
                pltpu.VMEM((padded, HEAD), jnp.float32),
                pltpu.VMEM((shares, width), jnp.int32),
                pltpu.VMEM((shares, width), jnp.float32),
                pltpu.VMEM((subs, wide, wide), jnp.float32),
            ],
        ),
        out_shape=jax.ShapeDtypeStruct((heads, subs, wide, wide), jnp.bfloat16),
        compiler_params=pltpu.CompilerParams(vmem_limit_bytes=VMEM_LIMIT),
        cost_estimate=pl.CostEstimate(
            flops=2 * heads * rows * wide * HEAD,
            bytes_accessed=4 * heads * rows * HEAD + 2 * heads * rows * wide,
            transcendentals=heads * rows * wide,
        ),
        name="temporal_weights",
    )(slots, counts, factors, frame, q_gain, k_gain, *[array for array, _, _ in far])


def mix_kernel(
    slots_ref, count_ref, scale_ref, weight_ref, *rest, count, each, part, more, skips, size, whole
):
    mixed, rest = rest[:count], rest[count:]
    weights, rest = rest[: -(count + 3 + more * count)], rest[-(count + 3 + more * count) :]
    before, rest = rest[: more * count], rest[more * count :]
    outs, (dot_ref, square_ref, rank_ref) = rest[:count], rest[count:]
    block = mixed[0].shape[1]

    def begin():
        dot_ref[...] = jnp.zeros_like(dot_ref)
        square_ref[...] = jnp.zeros_like(square_ref)
        store_shares(count_ref, rank_ref)

    if whole:
        begin()
    else:
        pl.when(pl.program_id(0) == 0)(begin)

    subs = [(ref, skip, j) for ref, skip in zip(weights, skips) for j in range(ref.shape[1])]
    for sub, (p_ref, skip, j) in enumerate(subs):
        at = sub * part
        dots = [dot_ref[slot, at : at + part] for slot in range(count)]
        squares = [square_ref[slot, at : at + part] for slot in range(count)]
        for h in range(size):
            o = jnp.concatenate([mixed[slot][h, at : at + part] for slot in range(count)], axis=0)
            t = jnp.dot(p_ref[skip + h, j], o, preferred_element_type=jnp.float32).astype(jnp.bfloat16)
            both = o.astype(jnp.float32) + t.astype(jnp.float32)
            for slot in range(count):
                m = both[slot * part : (slot + 1) * part] * scale_ref[skips[-1] + h, slot : slot + 1]
                dots[slot] = dots[slot] + m * weight_ref[skips[-1] + h]
                squares[slot] = squares[slot] + m * m
        for slot in range(count):
            dot_ref[slot, at : at + part] = dots[slot]
            square_ref[slot, at : at + part] = squares[slot]

    def end():
        hit = jnp.where(picks(rank_ref, slots_ref[0], each, 0, block), 1.0, 0.0)
        sums = [
            lane_sums(ref[slots_ref[count + i]])
            for i in range(count)
            for ref in (dot_ref, square_ref)
        ]
        sums = jnp.concatenate(sums, axis=0)
        high = sums.astype(jnp.bfloat16).astype(jnp.float32)
        middle = (sums - high).astype(jnp.bfloat16).astype(jnp.float32)
        terms = jnp.concatenate([high, middle, sums - high - middle], axis=0)
        terms = jnp.dot(
            terms.astype(jnp.bfloat16),
            hit.astype(jnp.bfloat16),
            preferred_element_type=jnp.float32,
        )
        number = 2 * count
        placed = terms[:number] + terms[number : 2 * number] + terms[2 * number :]
        for i, out in enumerate(outs):
            mine = placed[2 * i : 2 * i + 2]
            out[...] = before[i][...] + mine if more else mine

    if whole:
        end()
    else:
        pl.when(pl.program_id(0) == pl.num_programs(0) - 1)(end)


def mix(slots, counts, weights, scales, weight, before, mixed, first, each, shares, part):
    count = len(mixed)
    size, block, _ = mixed[0].shape
    wide = count * part
    rows = count * block
    width = counts.size // shares
    step = max(i for i in range(1, 6) if size % i == 0 and first % i == 0)
    skip = first // step
    whole = len(before) > 0 and size == step
    skips = tuple(first - at if whole else 0 for _, at in weights)
    skips += (first if whole else 0,)
    kernel = functools.partial(
        mix_kernel,
        count=count,
        each=each,
        part=part,
        more=len(before) // count,
        skips=skips,
        size=step,
        whole=whole,
    )
    scratch = [
        pltpu.VMEM((count, block, HEAD), jnp.float32),
        pltpu.VMEM((count, block, HEAD), jnp.float32),
        pltpu.VMEM((shares, width), jnp.int32),
    ]
    operands = (slots, counts, scales, weight, *mixed, *[p for p, _ in weights], *before)
    if whole:
        held = pl.BlockSpec(memory_space=pltpu.VMEM)
        layout = {
            "in_specs": [pl.BlockSpec(memory_space=pltpu.SMEM)] + [held] * (len(operands) - 1),
            "out_specs": [held] * count,
            "scratch_shapes": scratch,
        }
    else:
        out = pl.BlockSpec((2, width), lambda h, s: (0, 0))
        layout = {
            "grid_spec": pltpu.PrefetchScalarGridSpec(
                num_scalar_prefetch=1,
                grid=(size // step,),
                in_specs=[
                    pl.BlockSpec(counts.shape, lambda h, s: (0, 0)),
                    pl.BlockSpec((step, count, HEAD), lambda h, s: (skip + h, 0, 0)),
                    pl.BlockSpec((step, 1, HEAD), lambda h, s: (skip + h, 0, 0)),
                ]
                + [pl.BlockSpec((step, block, HEAD), lambda h, s: (h, 0, 0))] * count
                + [
                    pl.BlockSpec(
                        (step, *p.shape[1:]),
                        lambda h, s, skip=(first - at) // step: (skip + h, 0, 0, 0),
                    )
                    for p, at in weights
                ]
                + [out] * len(before),
                out_specs=[out] * count,
                scratch_shapes=scratch,
            )
        }
    return pl.pallas_call(
        kernel,
        **layout,
        out_shape=[jax.ShapeDtypeStruct((2, width), jnp.float32)] * count,
        compiler_params=pltpu.CompilerParams(vmem_limit_bytes=VMEM_LIMIT),
        cost_estimate=pl.CostEstimate(
            flops=2 * size * rows * wide * HEAD,
            bytes_accessed=2 * size * rows * (HEAD + wide),
            transcendentals=0,
        ),
        name="temporal_mix",
    )(*operands)


def on_device(
    projected, q_gain, k_gain, head_weight, step_scale, timestep, frame_count, *, count, shares
):
    x = jnp.transpose(projected[0], (1, 2, 0, 3))
    heads, pixels = x.shape[1], x.shape[2]
    block, width, each = pixels // count, pixels // shares, count // shares
    part = 16
    sure = min(block, -(-13 * block // (16 * part)) * part)
    me = lax.axis_index("tm")
    slots = me ^ jnp.arange(count, dtype=jnp.int32)
    counts = frame_count.reshape(pixels // HEAD, HEAD)
    gains = (q_gain[:, None, :], k_gain[:, None, :])

    def swap(value, offset):
        return lax.ppermute(value, "tm", [(i, i ^ offset) for i in range(count)])

    first = heads * 4 // 5 if heads % 20 == 0 else heads
    ranges = [(at, size) for at, size in ((0, first), (first, heads - first)) if size]
    diagonal = {}
    after = slots
    for at, size in reversed(ranges):
        (piece,) = gather(after, counts, x, [count - 1], each, shares, 0, sure, at, size)
        diagonal[at] = swap(piece, count - 1)
        after = lax.optimization_barrier((slots, piece))[0]
    near = range(1, count - 1)
    *pieces, own, sums = gather(
        after, counts, x, [*near, 0], each, shares, 0, sure, 0, heads, True
    )
    sent = [swap(piece, i + 1) for i, piece in enumerate(pieces)]
    totals = lax.psum(sums, "space")
    factors = lax.rsqrt(totals / CHANNELS + EPSILON)

    groups = []
    for at, size in ranges:
        outs = spatial(slots, counts, x, factors, *gains, at, size, count, each, shares)
        groups.append((at, list(outs)))
    last = groups[-1][1][0]

    crowd = jnp.sum((frame_count.reshape(shares, width) >= 2).astype(jnp.float32), axis=1)
    crowd = jnp.max(crowd)
    early = diagonal[ranges[-1][0]]
    *sent, last = lax.optimization_barrier((*sent, *diagonal.values(), last))
    diagonal = dict(zip(diagonal, sent[len(near) :]))
    ready = sent
    far = {}
    for at, size in ranges:
        far[at] = [(pair, place, at) for pair in (own, *sent[: len(near)]) for place in range(2)]
        far[at] += [(diagonal[at], place, 0) for place in range(2)]
    mine = position_factors([(far[at], size) for at, size in ranges])
    weights = {
        at: [
            (
                temporal_weights(
                    slots, counts, mine, far[at], *gains, each, shares, 0, part, at, size
                ),
                at,
            )
        ]
        for at, size in ranges
    }
    p = weights[0][0][0]
    if sure < block:

        def exchanged():
            spare = gather(
                slots, counts, x, range(count), each, shares, sure, block - sure, 0, heads
            )
            spare = lax.all_to_all(jnp.stack(spare)[slots], "tm", 0, 0)[slots]
            spare = [(spare[slot], place, 0) for slot in range(count) for place in range(2)]
            scale = position_factors([(spare, heads)])
            return temporal_weights(
                slots, counts, scale, spare, *gains, each, shares, sure, part, 0, heads
            )

        def single():
            wide = count * part
            row = lax.broadcasted_iota(jnp.int32, (wide, wide), 0)
            column = lax.broadcasted_iota(jnp.int32, (wide, wide), 1)
            hit = ((row - column) % part == 0) & (column // part == me)
            return jnp.broadcast_to(
                hit.astype(jnp.bfloat16), (heads, (block - sure) // part, wide, wide)
            )

        others = lax.cond(crowd > float(sure * each), exchanged, single)
        for at, _ in ranges:
            weights[at].append((others, 0))

    scales = jnp.transpose(step_scale[timestep[slots]], (1, 0, 2))
    weight = head_weight[:, None, :]
    sends = [(outs, offset) for _, outs in groups for offset in range(1, count)]
    for i, (outs, offset) in enumerate(sends):
        after = (early,) if i < 2 else ready if i < 5 else (p,)
        outs[offset] = lax.optimization_barrier((outs[offset], *after))[0]

    core = lax.axis_index("space")
    rounds = [(r, u) for r in range(each) for u in range(shares)]
    frames = [(core - u) % shares * each + (me - r) % each for r, u in rounds]
    order = jnp.concatenate([slots, me ^ jnp.stack(frames)])
    total = []
    for at, outs in groups:
        mixed = [outs[0]] + [swap(outs[offset], offset) for offset in range(1, count)]
        total = mix(
            order, counts, weights[at], scales, weight, total, mixed, at, each, shares, part
        )
    logits = jnp.zeros((width,), jnp.float32)
    for r in range(each):
        sums = jnp.zeros((2, width), jnp.float32)
        for u in range(shares):
            pairs = [
                (
                    (s * each + (f + r) % each) * shares + (f // each + u) % shares,
                    f * shares + s,
                )
                for f in range(count)
                for s in range(shares)
            ]
            sums = sums + lax.ppermute(total[r * shares + u], ("tm", "space"), pairs)
        logits = logits + sums[0] * lax.rsqrt(sums[1] / CHANNELS + EPSILON)
    return logits[None, :]


def solution(mesh):
    in_specs = (
        P(("dp", "tm"), None, None, "space", None),
        P("space", None),
        P("space", None),
        P("space", None),
        P(None, "space", None),
        P("dp"),
        P("dp"),
    )
    return jax.shard_map(
        functools.partial(on_device, count=mesh.shape["tm"], shares=mesh.shape["space"]),
        mesh=mesh,
        in_specs=in_specs,
        out_specs=P(("dp", "tm"), "space"),
        check_vma=False,
    )
```
